256 devices in a mesh: ctx: 32 (over x, z), head: 8 (over y, core).
Axes of the slice: x: 4, y: 4, z: 8, core: 2. Of those that a mesh axis runs over, the one named last changes fastest.
Arguments:
- tokens: bfloat16 [256, 4096], P(None, 'ctx'), may hold values from -400 to 400
- input_norm_gain: bfloat16 [4096], P('ctx'), may hold values from 0.099609375 to 1.8984375
- query_matrix: bfloat16 [4096, 4096], P('ctx', 'head'), may hold values from -0.09375 to 0.09375
- key_matrix: bfloat16 [4096, 1024], P('ctx', 'head'), may hold values from -0.09375 to 0.09375
- value_matrix: bfloat16 [4096, 1024], P('ctx', 'head'), may hold values from -0.09375 to 0.09375
- output_matrix: bfloat16 [4096, 4096], P('head', 'ctx'), may hold values from -0.09375 to 0.09375
- cached_key_rows: bfloat16 [262144, 1024], P('ctx', 'head'), may hold values from -64 to 64
- cached_value_rows: bfloat16 [262144, 1024], P('ctx', 'head'), may hold values from -6 to 6
- cache_block_recording: int32 [2048], P('ctx'), may hold values from 0 to 63, never falling along the last dimension, each value on 1 to 128 neighbouring positions
- stretch_token_recording: int32 [256], replicated, may hold values from 0 to 63, never falling along the last dimension, each value on 1 to 16 neighbouring positions
- adapter_down_store: bfloat16 [64, 64, 4096], P('ctx'), may hold values from -0.09375 to 0.09375
- adapter_up_store: bfloat16 [64, 64, 4096], P('ctx', None, 'head'), may hold values from -0.75 to 0.75
- adapter_store_slot: int32 [64], replicated, may hold values from 0 to 63, each once
- adapter_wanted_list: int32 [4], replicated, may hold values from 0 to 63, as said below
- token_adapter_place: int32 [256], replicated, may hold values from 0 to 3
Outputs:
- mixed_out: bfloat16 [256, 4096], P('head', 'ctx')
The draws below stay inside these ranges and needn't reach their ends.
Inputs may be any that keep to these rules, and one draw needn't show every extreme that they name: `cache_block_recording`: the recording of each block of 128 cache tokens; it never falls along the cache and every recording has at least one block. `stretch_token_recording`: never falls along the stretch and every recording has at least one stretch token. `adapter_store_slot`: store slot s lies at ctx index s // 2, place s % 2 of that index's store; every slot once. `adapter_wanted_list`: distinct adapter ids.
All inputs are finite; a program needn't handle non-finite values.
Results may differ from the reference program's by a relative error of at most 0.011.
The reference program's roundings to bfloat16 on the way count: a program that leaves them out, or rounds other values in their place, can miss the bound.
Values may be sent and summed in bfloat16 or wider, within the bound.
No kernel may reach another device: no remote copies, remote signals or barrier semaphores. Data moves between devices by JAX's collectives and lax.ppermute only.
A program may use at most 64 MiB of HBM per device.

```python
import math
import jax
import jax.numpy as jnp
import numpy as np
from jax import lax

MODEL_WIDTH = 4096
QUERY_HEADS = 32
KVH = 8
HEAD_WIDTH = 128
ADAPTER_RANK = 64
SPAN = 128
NEED = 4
STRETCH = 256
CTX_DEV = 8192
GROUP = 4
CTX = 262144
BLOCKS = 2048
RECORDS = 64
ADAPTER_TOTAL = 64
N_CTX = 32


def draw_tokens(key, part):
    key = jax.random.fold_in(key, 2)
    first_key, second_key = jax.random.split(key, 2)
    rising = 1.0 + 2.0 * jnp.arange(MODEL_WIDTH, dtype=jnp.float32) / (MODEL_WIDTH - 1)
    base = jnp.clip(jax.random.normal(first_key, (STRETCH, MODEL_WIDTH), jnp.float32), -6.0, 6.0)
    row_scale = jnp.exp(jax.random.uniform(second_key, (STRETCH, 1), jnp.float32, 0.0, jnp.log(10.0)))
    return (base * rising[None, :] * row_scale).astype(jnp.bfloat16)


def draw_cached_key_rows(key, part):
    key = jax.random.fold_in(key, 3)
    first_key = jax.random.fold_in(key, 0)
    return jnp.clip(jax.random.normal(first_key, (CTX, KVH * HEAD_WIDTH), jnp.float32), -6.0, 6.0).astype(jnp.bfloat16)


def draw_adapter_wanted_list(key, part):
    key = jax.random.fold_in(key, 5)
    first_key, second_key = jax.random.split(key, 2)
    inner = jax.random.permutation(first_key, ADAPTER_TOTAL - 2)[:NEED - 2].astype(jnp.int32) + 1
    ends = jnp.array([0, ADAPTER_TOTAL - 1], jnp.int32)
    whole = jnp.concatenate([ends, inner])
    return whole[jax.random.permutation(second_key, NEED)].astype(jnp.int32)


def with_ends(values, key, least, top_value):
    extent = values.shape
    place = [jax.random.randint(jax.random.fold_in(key, axis), (), 0, extent[axis]) for axis in range(len(extent))]
    values = values.at[tuple(place)].set(least)
    longest = extent.index(max(extent))
    place[longest] = (place[longest] + 1) % extent[longest]
    return values.at[tuple(place)].set(top_value)


def shard_levels(rng, shape, shards, smallest, top_value):
    level = 1.0
    for dim, parts in shards:
        draws = jax.random.uniform(jax.random.fold_in(jax.random.fold_in(rng, 6), dim), (parts,), jnp.float32, smallest / len(shards), top_value / len(shards))
        level = level * jnp.repeat(jnp.exp(draws), shape[dim] // parts).reshape((-1,) + (1,) * (len(shape) - 1 - dim))
    return level


def length_profile(number_of, total, reach, lean):
    weights = [(1 << 20) // math.isqrt(grade ** lean) + 1 for grade in range(2, number_of + 1)]
    surplus, counts = total - reach - (number_of - 1), [1] * (number_of - 1)
    while surplus > 0:
        movable = [i for i in range(number_of - 1) if counts[i] < reach]
        mass, remaining = sum([weights[i] for i in movable]), surplus
        for i in movable:
            more = min(reach - counts[i], max(1, remaining * weights[i] // mass), surplus)
            counts[i] = counts[i] + more
            surplus = surplus - more
    return np.array([reach] + counts)


def ragged_sizes(rng, number_of, total, reach, slope):
    if number_of == 2:
        one = jax.random.randint(rng, (), max(1, total - reach), min(reach, total - 1) + 1)
        return jnp.stack([one, total - one])
    sizes = jnp.asarray(length_profile(number_of, total, reach, slope), jnp.int32)
    pairs = (number_of - 1) // 2
    source_of, sink = sizes[1:1 + 2 * pairs:2], sizes[2:2 + 2 * pairs:2]
    margin = jnp.minimum(source_of - 1, reach - sink)
    passed = jax.random.randint(jax.random.fold_in(rng, 1), (pairs,), 0, 1 << 20) % (margin + 1)
    sizes = sizes.at[1:1 + 2 * pairs:2].set(source_of - passed).at[2:2 + 2 * pairs:2].set(sink + passed)
    return sizes[jax.random.permutation(jax.random.fold_in(rng, 2), number_of)]


def bell_draw(key, dims, deviation, reach, shards=(), kind=jnp.bfloat16):
    gain = shard_levels(key, dims, shards, -0.22, 0.18) if shards else 1.0
    values = jax.random.normal(key, dims, jnp.float32) * deviation * gain
    return jnp.minimum(jnp.maximum(values, -reach), reach).astype(kind)


def setup_inputs(seed: int = 0) -> dict:
    key_list = jax.random.split(jax.random.key(seed), 16)
    return {
        "tokens": draw_tokens(jax.random.fold_in(key_list[15], 71), 0),
        "input_norm_gain": jnp.clip(1.0 + 0.18 * jax.random.normal(key_list[1], (MODEL_WIDTH,), jnp.float32), 0.099609375, 1.8984375).astype(jnp.bfloat16),
        "query_matrix": bell_draw(key_list[2], (MODEL_WIDTH, QUERY_HEADS * HEAD_WIDTH), MODEL_WIDTH ** -0.5, 0.09375, ((0, 32), (1, 8))),
        "key_matrix": bell_draw(key_list[3], (MODEL_WIDTH, KVH * HEAD_WIDTH), MODEL_WIDTH ** -0.5, 0.09375, ((0, 32), (1, 8))),
        "value_matrix": bell_draw(key_list[4], (MODEL_WIDTH, KVH * HEAD_WIDTH), MODEL_WIDTH ** -0.5, 0.09375, ((0, 32), (1, 8))),
        "output_matrix": bell_draw(key_list[5], (QUERY_HEADS * HEAD_WIDTH, MODEL_WIDTH), (QUERY_HEADS * HEAD_WIDTH) ** -0.5, 0.09375, ((0, 8), (1, 32))),
        "cached_key_rows": draw_cached_key_rows(jax.random.fold_in(key_list[15], 71), 0),
        "cached_value_rows": bell_draw(key_list[7], (CTX, KVH * HEAD_WIDTH), 1.0, 6.0, ((0, 32), (1, 8))),
        "cache_block_recording": jnp.searchsorted(jnp.cumsum(ragged_sizes(key_list[8], RECORDS, BLOCKS, 4 * BLOCKS // RECORDS, 2)), jnp.arange(BLOCKS), side="right").astype(jnp.int32),
        "stretch_token_recording": jnp.searchsorted(jnp.cumsum(ragged_sizes(key_list[9], RECORDS, STRETCH, 4 * STRETCH // RECORDS, 2)), jnp.arange(STRETCH), side="right").astype(jnp.int32),
        "adapter_down_store": bell_draw(key_list[10], (ADAPTER_TOTAL, ADAPTER_RANK, MODEL_WIDTH), MODEL_WIDTH ** -0.5, 0.09375, ((0, 32),)),
        "adapter_up_store": bell_draw(key_list[11], (ADAPTER_TOTAL, ADAPTER_RANK, QUERY_HEADS * HEAD_WIDTH), ADAPTER_RANK ** -0.5, 0.75, ((0, 32), (2, 8))),
        "adapter_store_slot": jax.random.permutation(key_list[12], ADAPTER_TOTAL).astype(jnp.int32),
        "adapter_wanted_list": draw_adapter_wanted_list(jax.random.fold_in(key_list[15], 71), 0),
        "token_adapter_place": with_ends(jax.random.randint(key_list[14], (STRETCH,), 0, NEED), jax.random.fold_in(key_list[14], 1), 0, NEED - 1).astype(jnp.int32),
    }


NEGATIVE = -1e+30
EPSILON = 1e-05
ADAPTER_SCALE = 0.5

def ref_attend(carried, query_tile, key_block, value_block, allowed):
    highest, mass_sum, numerator = carried
    scores = jnp.einsum('qhgd,khd->hgqk', query_tile.astype(jnp.float32), key_block.astype(jnp.float32)) * (1.0 / math.sqrt(HEAD_WIDTH))
    scores = jnp.where(allowed[None, None], scores, NEGATIVE)
    peak_new = jnp.maximum(highest, lax.optimization_barrier(jnp.max(scores, axis=-1)))
    factor = jnp.exp(highest - peak_new)
    weights = jnp.where(allowed[None, None], jnp.exp(scores - peak_new[..., None]), 0.0)
    mass_sum = mass_sum * factor + lax.optimization_barrier(jnp.sum(weights, axis=-1))
    rounded = weights.astype(jnp.bfloat16).astype(jnp.float32)
    numerator = numerator * jnp.transpose(factor, (2, 0, 1))[..., None] + jnp.einsum('hgqk,khd->qhgd', rounded, value_block.astype(jnp.float32))
    return (peak_new, mass_sum, numerator)

def reference(tokens, input_norm_gain, query_matrix, key_matrix, value_matrix, output_matrix, cached_key_rows, cached_value_rows, cache_block_recording, stretch_token_recording, adapter_down_store, adapter_up_store, adapter_store_slot, adapter_wanted_list, token_adapter_place):
    float_tokens = tokens.astype(jnp.float32)
    inverse_root_square = lax.rsqrt(lax.optimization_barrier(jnp.sum(float_tokens * float_tokens, axis=1)) / MODEL_WIDTH + EPSILON)
    scaled_change = (float_tokens * input_norm_gain.astype(jnp.float32)).astype(jnp.bfloat16)
    slot_hits = token_adapter_place[:, None] == jnp.arange(NEED, dtype=jnp.int32)[None, :]
    store_list = adapter_store_slot[adapter_wanted_list]
    down_map_list = adapter_down_store[store_list]
    up_map_list = adapter_up_store[store_list]
    middle = jnp.zeros((STRETCH, ADAPTER_RANK), jnp.float32)
    for wanted_index in range(NEED):
        product = jnp.dot(scaled_change, down_map_list[wanted_index].T, preferred_element_type=jnp.float32)
        middle = middle + jnp.where(slot_hits[:, wanted_index:wanted_index + 1], product, 0.0)
    middle = (middle * inverse_root_square[:, None]).astype(jnp.bfloat16)
    query_change = jnp.zeros((STRETCH, QUERY_HEADS * HEAD_WIDTH), jnp.float32)
    for wanted_index in range(NEED):
        product = jnp.dot(middle, up_map_list[wanted_index], preferred_element_type=jnp.float32)
        query_change = query_change + jnp.where(slot_hits[:, wanted_index:wanted_index + 1], product, 0.0)
    query_vectors = (jnp.dot(scaled_change, query_matrix, preferred_element_type=jnp.float32) * inverse_root_square[:, None] + ADAPTER_SCALE * query_change).astype(jnp.bfloat16)
    new_keys = (jnp.dot(scaled_change, key_matrix, preferred_element_type=jnp.float32) * inverse_root_square[:, None]).astype(jnp.bfloat16)
    new_values = (jnp.dot(scaled_change, value_matrix, preferred_element_type=jnp.float32) * inverse_root_square[:, None]).astype(jnp.bfloat16)
    positions = jnp.arange(STRETCH, dtype=jnp.int32)
    stretch_allowed = (stretch_token_recording[:, None] == stretch_token_recording[None, :]) & (positions[None, :] <= positions[:, None])
    record_blocks = jnp.repeat(cache_block_recording, SPAN).reshape(N_CTX, CTX_DEV)
    query_heads = query_vectors.reshape(STRETCH, KVH, GROUP, HEAD_WIDTH).transpose(1, 0, 2, 3)[:, :, None]
    cache_keys = cached_key_rows.reshape(N_CTX, CTX_DEV, KVH, HEAD_WIDTH).transpose(2, 0, 1, 3)[:, :, :, None]
    cache_values = cached_value_rows.reshape(N_CTX, CTX_DEV, KVH, HEAD_WIDTH).transpose(2, 0, 1, 3)[:, :, :, None]
    stretch_keys = new_keys.reshape(STRETCH, KVH, HEAD_WIDTH).transpose(1, 0, 2)[:, :, None]
    stretch_values = new_values.reshape(STRETCH, KVH, HEAD_WIDTH).transpose(1, 0, 2)[:, :, None]

    def one_head(inputs):
        query_one, keys_one, values_one, knew_one, vnew_one = inputs
        carried = (jnp.full((1, GROUP, STRETCH), NEGATIVE, jnp.float32), jnp.zeros((1, GROUP, STRETCH), jnp.float32), jnp.zeros((STRETCH, 1, GROUP, HEAD_WIDTH), jnp.float32))

        def cache_step(carry_in, blocks):
            key_block, value_block, record_block = blocks
            allowed = stretch_token_recording[:, None] == record_block[None, :]
            return (ref_attend(carry_in, query_one, key_block, value_block, allowed), None)
        carried, unused = lax.scan(cache_step, carried, (keys_one, values_one, record_blocks))
        carried = ref_attend(carried, query_one, knew_one, vnew_one, stretch_allowed)
        highest, mass_sum, numerator = carried
        return (numerator / jnp.transpose(mass_sum, (2, 0, 1))[..., None]).reshape(STRETCH, GROUP * HEAD_WIDTH)
    per_head = lax.map(one_head, (query_heads, cache_keys, cache_values, stretch_keys, stretch_values))
    attention = per_head.transpose(1, 0, 2).reshape(STRETCH, QUERY_HEADS * HEAD_WIDTH).astype(jnp.bfloat16)
    return jnp.dot(attention, output_matrix, preferred_element_type=jnp.float32).astype(jnp.bfloat16)
```

```python
import math

import jax
import jax.numpy as jnp
from jax import lax
from jax.experimental import pallas as pl
from jax.experimental.pallas import tpu as pltpu
from jax.sharding import PartitionSpec as P

MODEL_WIDTH = 4096
HEAD_WIDTH = 128
LANES = 128
SPAN = 128
NEED = 4
GROUP = 4
RANK = 64
WINDOW = 24

LOWEST = -1e30
FLOOR = -1e29
EPSILON = 1e-05
ADAPTER_SCALE = 0.5
SCORE_SCALE = math.log2(math.e) / math.sqrt(HEAD_WIDTH)

F32 = jnp.float32
BF16 = jnp.bfloat16
VMEM = pl.BlockSpec(memory_space=pltpu.VMEM)
SMEM = pl.BlockSpec(memory_space=pltpu.SMEM)


def lane_iota(shape):
    return lax.broadcasted_iota(jnp.int32, shape, len(shape) - 1)


def row_iota(shape):
    return lax.broadcasted_iota(jnp.int32, shape, len(shape) - 2)


def column_of(row):
    return jnp.transpose(jnp.broadcast_to(row.astype(F32), (LANES, LANES)))


def thirds(value):
    high = value.astype(BF16).astype(F32)
    rest = value - high
    middle = rest.astype(BF16).astype(F32)
    return high, middle, rest - middle


def contract_last(a, b):
    return lax.dot_general(a, b, (((1,), (1,)), ((), ())), preferred_element_type=F32)


def call(body, out_shape, in_specs, scratch=(), limit=16, flops=0, name=None):
    many = isinstance(out_shape, (tuple, list))
    return pl.pallas_call(
        body,
        out_shape=out_shape,
        in_specs=in_specs,
        out_specs=[VMEM] * len(out_shape) if many else VMEM,
        scratch_shapes=list(scratch),
        compiler_params=pltpu.CompilerParams(vmem_limit_bytes=limit * 1024 * 1024),
        name=name,
    )


def pack_tokens(tokens, gain, out):
    rows = out.shape[1] - 8
    first = pl.multiple_of(lax.axis_index("head") * rows, rows)
    own = tokens[pl.ds(first, rows), :].astype(F32)
    gain_rows = jnp.broadcast_to(gain[...].astype(F32), (8, LANES))
    block = jnp.concatenate([own, gain_rows], axis=0).astype(BF16)
    for target in range(out.shape[0]):
        out[target] = block


def middle_kernel(
    wanted, store_slot, blocks, down, place, stretch, cache, out, table, flat, place_columns
):
    rows = flat.shape[0]
    first_home = lax.axis_index("ctx") * 2
    squares = jnp.zeros((rows, LANES), F32)
    for source in range(blocks.shape[0]):
        block = blocks[source].astype(F32)
        token_part = block[:rows]
        squares = squares + token_part * token_part
        scaled = (token_part * block[rows : rows + 1]).astype(BF16)
        flat[:, source * LANES : (source + 1) * LANES] = scaled
    mean = jnp.sum(squares, axis=1, keepdims=True) / MODEL_WIDTH
    inverse = lax.rsqrt(mean + EPSILON)
    middle = contract_last(flat[...], down[...]) * inverse
    head = lax.axis_index("head")
    for part in range(place.shape[0]):
        place_columns[part * LANES : (part + 1) * LANES, :] = column_of(place[part : part + 1, :])
    own_place = place_columns[pl.ds(pl.multiple_of(head * rows, rows), rows), :]
    use_first = jnp.zeros((rows, LANES), jnp.bool_)
    use_second = jnp.zeros((rows, LANES), jnp.bool_)
    for wanted_index in range(NEED):
        home = store_slot[wanted[wanted_index]]
        here = own_place == float(wanted_index)
        use_first = use_first | (here & (home == first_home))
        use_second = use_second | (here & (home == first_home + 1))
    picked = jnp.where(
        use_first, middle, jnp.where(use_second, pltpu.roll(middle, RANK, 1), 0.0)
    )
    lanes = lane_iota((rows, LANES))
    high, mid, low = thirds(jnp.broadcast_to(inverse, (rows, LANES)))
    tail = jnp.where(
        lanes == RANK, high, jnp.where(lanes == RANK + 1, mid, jnp.where(lanes == RANK + 2, low, 0.0))
    )
    packed = jnp.where(lanes < RANK, picked, tail).astype(BF16)
    for target in range(out.shape[0]):
        out[target] = packed
    cache_row = jnp.broadcast_to(cache[...].astype(F32), (LANES, LANES))
    counts = [jnp.zeros((1, LANES), F32) for _ in range(2 + stretch.shape[0])]
    for part in range(stretch.shape[0]):
        column = column_of(stretch[part : part + 1, :])
        counts[0] = counts[0] + jnp.sum(jnp.where(column < cache_row, 1.0, 0.0), axis=0, keepdims=True)
        counts[1] = counts[1] + jnp.sum(jnp.where(column <= cache_row, 1.0, 0.0), axis=0, keepdims=True)
        for other in range(stretch.shape[0]):
            other_row = jnp.broadcast_to(stretch[other : other + 1, :].astype(F32), (LANES, LANES))
            counts[2 + other] = counts[2 + other] + jnp.sum(
                jnp.where(column < other_row, 1.0, 0.0), axis=0, keepdims=True
            )
    rows_out = jnp.concatenate(counts + [jnp.zeros((8 - len(counts), LANES), F32)], axis=0)
    table[...] = rows_out.astype(jnp.int32)


def project_kernel(
    wanted, store_slot, tokens, gain, middles, place, query_matrix, key_matrix, value_matrix, up, out
):
    total_rows = tokens.shape[0]
    first_home = lax.axis_index("ctx") * 2
    scaled = (tokens[...].astype(F32) * gain[...].astype(F32)).astype(BF16)
    packed = middles[...].astype(F32)
    lanes = lane_iota((total_rows, LANES))
    inverse = jnp.sum(
        jnp.where((lanes >= RANK) & (lanes < RANK + 3), packed, 0.0), axis=1, keepdims=True
    )
    place_column = jnp.concatenate(
        [column_of(place[part : part + 1, :]) for part in range(place.shape[0])], axis=0
    )
    use_first = jnp.zeros((total_rows, LANES), jnp.bool_)
    use_second = jnp.zeros((total_rows, LANES), jnp.bool_)
    for wanted_index in range(NEED):
        home = store_slot[wanted[wanted_index]]
        here = place_column == float(wanted_index)
        use_first = use_first | (here & (home == first_home))
        use_second = use_second | (here & (home == first_home + 1))
    spread = jnp.where(
        lanes < RANK,
        jnp.where(use_first, packed, 0.0),
        jnp.where(use_second, pltpu.roll(packed, RANK, 1), 0.0),
    ).astype(BF16)
    query_columns = query_matrix.shape[1]
    change = jnp.dot(spread, up[...], preferred_element_type=F32)
    query = jnp.dot(scaled, query_matrix[...], preferred_element_type=F32)
    out[:, :query_columns] = (query * inverse + ADAPTER_SCALE * change).astype(BF16)
    key = jnp.dot(scaled, key_matrix[...], preferred_element_type=F32)
    out[:, query_columns : query_columns + LANES] = (key * inverse).astype(BF16)
    value = jnp.dot(scaled, value_matrix[...], preferred_element_type=F32)
    out[:, query_columns + LANES :] = (value * inverse).astype(BF16)


def sum_kernel(parts, out):
    total = parts[0].astype(F32)
    for source in range(1, parts.shape[0]):
        total = total + parts[source].astype(F32)
    total = total.astype(BF16)
    for target in range(out.shape[0]):
        out[target] = total


def attention_kernel(table, vectors, keys, values, out, queries, peaks, masses, sums, scores):
    total_rows = vectors.shape[0]
    own_rows = 8
    block_count = keys.shape[0] // SPAN
    head_columns = GROUP * HEAD_WIDTH
    tall = GROUP * WINDOW
    window_row = row_iota((tall, LANES))
    window_row = window_row - WINDOW * (window_row // WINDOW)

    for g in range(GROUP):
        queries[g] = vectors[:, g * HEAD_WIDTH : (g + 1) * HEAD_WIDTH].astype(F32)
    peaks[...] = jnp.full(peaks.shape, LOWEST, F32)
    masses[...] = jnp.zeros(masses.shape, F32)
    sums[...] = jnp.zeros(sums.shape, F32)

    def window_of(block):
        begin = table[0, block]
        start = jnp.minimum((begin // 8) * 8, total_rows - WINDOW)
        return pl.multiple_of(start, 8), begin, table[1, block]

    def load(ref, start, length):
        return jnp.concatenate([ref[g, pl.ds(start, length), :] for g in range(GROUP)], axis=0)

    own_first = pl.multiple_of(lax.axis_index("ctx") * own_rows, own_rows)
    own_shape = (GROUP * own_rows, total_rows)
    own_row = row_iota(own_shape)
    own_row = own_row - own_rows * (own_row // own_rows)
    key_position = lane_iota(own_shape)
    fellow = jnp.zeros(own_shape, jnp.int32)
    for j in range(own_rows):
        position = own_first + j
        fellow = jnp.where(own_row == j, table[2 + position // LANES, position % LANES], fellow)
    own_allowed = (key_position >= fellow) & (key_position <= own_row + own_first)
    new_keys = vectors[:, head_columns : head_columns + HEAD_WIDTH]
    new_values = vectors[:, head_columns + HEAD_WIDTH :]
    own_queries = load(queries, own_first, own_rows).astype(BF16)
    own_scores = jnp.where(own_allowed, contract_last(own_queries, new_keys) * SCORE_SCALE, LOWEST)
    own_peak = own_scores[:, :LANES]
    for part in range(1, total_rows // LANES):
        own_peak = jnp.maximum(own_peak, own_scores[:, part * LANES : (part + 1) * LANES])
    for g in range(GROUP):
        peaks[g, pl.ds(own_first, own_rows), :] = own_peak[g * own_rows : (g + 1) * own_rows]

    unroll = 8

    def score_step(step, carry):
        found = []
        for k in range(unroll):
            block = step * unroll + k
            start, begin, end = window_of(block)
            key_block = keys[pl.ds(pl.multiple_of(block * SPAN, SPAN), SPAN), :]
            result = contract_last(load(queries, start, WINDOW).astype(BF16), key_block)
            position = window_row + start
            allowed = (position >= begin) & (position < end)
            result = jnp.where(allowed, result * SCORE_SCALE, LOWEST)
            scores[block] = result
            found.append((start, result))
        for start, result in found:
            for g in range(GROUP):
                place = pl.ds(start, WINDOW)
                peaks[g, place, :] = jnp.maximum(
                    peaks[g, place, :], result[g * WINDOW : (g + 1) * WINDOW]
                )
        return carry

    lax.fori_loop(0, block_count // unroll, score_step, 0)
    for g in range(GROUP):
        highest = jnp.max(peaks[g], axis=1, keepdims=True)
        peaks[g] = jnp.broadcast_to(jnp.maximum(highest, FLOOR), (total_rows, LANES))

    own_highest = load(peaks, own_first, own_rows)
    own_weights = jnp.concatenate(
        [
            jnp.exp2(own_scores[:, part * LANES : (part + 1) * LANES] - own_highest)
            for part in range(total_rows // LANES)
        ],
        axis=1,
    )
    own_mass = own_weights[:, :LANES]
    for part in range(1, total_rows // LANES):
        own_mass = own_mass + own_weights[:, part * LANES : (part + 1) * LANES]
    own_sum = jnp.dot(own_weights.astype(BF16), new_values, preferred_element_type=F32)
    for g in range(GROUP):
        masses[g, pl.ds(own_first, own_rows), :] = own_mass[g * own_rows : (g + 1) * own_rows]
        sums[g, pl.ds(own_first, own_rows), :] = own_sum[g * own_rows : (g + 1) * own_rows]

    def value_step(step, carry):
        found = []
        for k in range(unroll):
            block = step * unroll + k
            start, begin, end = window_of(block)
            weights = jnp.exp2(scores[block] - load(peaks, start, WINDOW))
            value_block = values[pl.ds(pl.multiple_of(block * SPAN, SPAN), SPAN), :]
            product = jnp.dot(weights.astype(BF16), value_block, preferred_element_type=F32)
            found.append((start, weights, product))
        for start, weights, product in found:
            for g in range(GROUP):
                place = pl.ds(start, WINDOW)
                rows = slice(g * WINDOW, (g + 1) * WINDOW)
                masses[g, place, :] = masses[g, place, :] + weights[rows]
                sums[g, place, :] = sums[g, place, :] + product[rows]
        return carry

    lax.fori_loop(0, block_count // unroll, value_step, 0)

    lanes = lane_iota((total_rows, LANES))
    quarter = lanes % GROUP
    peak_all = jnp.zeros((total_rows, LANES), F32)
    mass_all = jnp.zeros((total_rows, LANES), F32)
    for g in range(GROUP):
        mass = jnp.sum(masses[g], axis=1, keepdims=True)
        scale = jnp.where(mass > 0.0, 1.0 / mass, 0.0)
        out[:, g * HEAD_WIDTH : (g + 1) * HEAD_WIDTH] = (sums[g] * scale).astype(BF16)
        peak_all = jnp.where(quarter == g, peaks[g], peak_all)
        mass_all = jnp.where(quarter == g, mass, mass_all)
    notes = jnp.zeros((total_rows, LANES), F32)
    for index, part in enumerate(thirds(peak_all) + thirds(mass_all)):
        inside = (lanes >= GROUP * index) & (lanes < GROUP * (index + 1))
        notes = jnp.where(inside, part, notes)
    out[:, head_columns:] = notes.astype(BF16)


def combine_kernel(parts, out):
    sources, own_rows, _ = parts.shape
    head_columns = GROUP * HEAD_WIDTH
    peaks = []
    masses = []
    for source in range(sources):
        notes = parts[source, :, head_columns:].astype(F32)

        def from_lane(index):
            if index == 0:
                return notes
            return pltpu.roll(notes, LANES - GROUP * index, 1)

        peaks.append(from_lane(0) + from_lane(1) + from_lane(2))
        masses.append(from_lane(3) + from_lane(4) + from_lane(5))
    highest = peaks[0]
    for source in range(1, sources):
        highest = jnp.maximum(highest, peaks[source])
    weights = [masses[s] * jnp.exp2(peaks[s] - highest) for s in range(sources)]
    total = weights[0]
    for source in range(1, sources):
        total = total + weights[source]
    results = [jnp.zeros((own_rows, HEAD_WIDTH), F32) for _ in range(GROUP)]
    for source in range(sources):
        share = weights[source] / total
        for g in range(GROUP):
            part = parts[source, :, g * HEAD_WIDTH : (g + 1) * HEAD_WIDTH].astype(F32)
            results[g] = results[g] + share[:, g : g + 1] * part
    block = jnp.concatenate(results, axis=1).astype(BF16)
    for target in range(out.shape[0]):
        out[target] = block


def shards(
    tokens,
    input_norm_gain,
    query_matrix,
    key_matrix,
    value_matrix,
    output_matrix,
    cached_key_rows,
    cached_value_rows,
    cache_block_recording,
    stretch_token_recording,
    adapter_down_store,
    adapter_up_store,
    adapter_store_slot,
    adapter_wanted_list,
    token_adapter_place,
):
    total_rows = tokens.shape[0]
    ctx_count = lax.axis_size("ctx")
    head_count = lax.axis_size("head")
    own_rows = total_rows // ctx_count
    head_rows = total_rows // head_count
    query_columns = query_matrix.shape[1]
    all_columns = query_columns + 2 * HEAD_WIDTH
    gain = input_norm_gain.reshape(1, LANES)
    place = token_adapter_place.reshape(total_rows // LANES, LANES)
    stretch = stretch_token_recording.reshape(total_rows // LANES, LANES)
    cache = jnp.pad(cache_block_recording, (0, LANES - cache_block_recording.shape[0])).reshape(1, LANES)
    down = adapter_down_store.reshape(2 * RANK, MODEL_WIDTH)
    up = adapter_up_store.reshape(2 * RANK, query_columns)

    packed = call(
        pack_tokens,
        jax.ShapeDtypeStruct((ctx_count, head_rows + 8, LANES), BF16),
        [VMEM, VMEM],
        name="pack_tokens",
    )(tokens, gain)
    blocks = lax.all_to_all(packed, "ctx", 0, 0, tiled=True)
    middles, table = call(
        middle_kernel,
        (
            jax.ShapeDtypeStruct((head_count, head_rows, LANES), BF16),
            jax.ShapeDtypeStruct((8, LANES), jnp.int32),
        ),
        [SMEM, SMEM] + [VMEM] * 5,
        [pltpu.VMEM((head_rows, MODEL_WIDTH), BF16), pltpu.VMEM((total_rows, LANES), F32)],
        name="adapter_middle",
    )(adapter_wanted_list, adapter_store_slot, blocks, down, place, stretch, cache)
    middles = lax.all_to_all(middles, "head", 0, 0, tiled=True).reshape(total_rows, LANES)
    partial = call(
        project_kernel,
        jax.ShapeDtypeStruct((total_rows, all_columns), BF16),
        [SMEM, SMEM] + [VMEM] * 8,
        name="project",
    )(
        adapter_wanted_list,
        adapter_store_slot,
        tokens,
        gain,
        middles,
        place,
        query_matrix,
        key_matrix,
        value_matrix,
        up,
    )
    partial = lax.all_to_all(
        partial.reshape(ctx_count, own_rows, all_columns), "ctx", 0, 0, tiled=True
    )
    vectors = call(
        sum_kernel,
        jax.ShapeDtypeStruct((ctx_count, own_rows, all_columns), BF16),
        [VMEM],
        name="sum_projections",
    )(partial)
    vectors = lax.all_to_all(vectors, "ctx", 0, 0, tiled=True).reshape(total_rows, all_columns)
    block_count = cached_key_rows.shape[0] // SPAN
    state = pltpu.VMEM((GROUP, total_rows, LANES), F32)
    parts = call(
        attention_kernel,
        jax.ShapeDtypeStruct((total_rows, query_columns + LANES), BF16),
        [SMEM] + [VMEM] * 3,
        [state, state, state, state, pltpu.VMEM((block_count, GROUP * WINDOW, LANES), F32)],
        limit=24,
        name="attention",
    )(table, vectors, cached_key_rows, cached_value_rows)
    parts = lax.all_to_all(
        parts.reshape(ctx_count, own_rows, query_columns + LANES), "ctx", 0, 0, tiled=True
    )
    attention = call(
        combine_kernel,
        jax.ShapeDtypeStruct((ctx_count, own_rows, query_columns), BF16),
        [VMEM],
        name="combine",
    )(parts)
    attention = lax.all_to_all(attention, "ctx", 0, 0, tiled=True).reshape(total_rows, query_columns)
    mixed = jnp.dot(attention, output_matrix, preferred_element_type=F32)
    mixed = lax.all_to_all(mixed.reshape(head_count, head_rows, LANES), "head", 0, 0, tiled=True)
    return jnp.sum(mixed, axis=0).astype(BF16)


def solution(mesh):
    in_specs = (
        P(None, "ctx"),
        P("ctx"),
        P("ctx", "head"),
        P("ctx", "head"),
        P("ctx", "head"),
        P("head", "ctx"),
        P("ctx", "head"),
        P("ctx", "head"),
        P("ctx"),
        P(),
        P("ctx", None, None),
        P("ctx", None, "head"),
        P(),
        P(),
        P(),
    )
    out_specs = P("head", "ctx")
    return jax.shard_map(shards, mesh=mesh, in_specs=in_specs, out_specs=out_specs, check_vma=False)
```

```python
import math

import jax
import jax.numpy as jnp
from jax import lax
from jax.experimental import pallas as pl
from jax.experimental.pallas import tpu as pltpu
from jax.sharding import PartitionSpec as P

MODEL_WIDTH = 4096
HEAD_WIDTH = 128
LANES = 128
SPAN = 128
NEED = 4
GROUP = 4
RANK = 64
WINDOW = 24

LOWEST = -1e30
FLOOR = -1e29
EPSILON = 1e-05
ADAPTER_SCALE = 0.5
SCORE_SCALE = math.log2(math.e) / math.sqrt(HEAD_WIDTH)

F32 = jnp.float32
BF16 = jnp.bfloat16
VMEM = pl.BlockSpec(memory_space=pltpu.VMEM)
SMEM = pl.BlockSpec(memory_space=pltpu.SMEM)
HBM = pl.BlockSpec(memory_space=pltpu.HBM)


def lane_iota(shape):
    return lax.broadcasted_iota(jnp.int32, shape, len(shape) - 1)


def row_iota(shape):
    return lax.broadcasted_iota(jnp.int32, shape, len(shape) - 2)


def column_of(row):
    return jnp.transpose(jnp.broadcast_to(row.astype(F32), (LANES, LANES)))


def thirds(value):
    high = value.astype(BF16).astype(F32)
    rest = value - high
    middle = rest.astype(BF16).astype(F32)
    return high, middle, rest - middle


def contract_last(a, b):
    return lax.dot_general(a, b, (((1,), (1,)), ((), ())), preferred_element_type=F32)


def call(body, out_shape, in_specs, scratch=(), limit=16, flops=0, name=None):
    many = isinstance(out_shape, (tuple, list))
    return pl.pallas_call(
        body,
        out_shape=out_shape,
        in_specs=in_specs,
        out_specs=[VMEM] * len(out_shape) if many else VMEM,
        scratch_shapes=list(scratch),
        compiler_params=pltpu.CompilerParams(vmem_limit_bytes=limit * 1024 * 1024),
        name=name,
    )


SLOT_ROW, WANTED_ROW = 0, 1


def home_of(numbers, wanted_index):
    return numbers[SLOT_ROW, numbers[WANTED_ROW, wanted_index]]


def pack_kernel(tokens_hbm, gain_hbm, out, tokens, gain, arrived):
    rows = tokens.shape[0]
    first = pl.multiple_of(lax.axis_index("head") * rows, rows)
    copies = [
        pltpu.make_async_copy(tokens_hbm.at[pl.ds(first, rows), :], tokens, arrived.at[0]),
        pltpu.make_async_copy(gain_hbm, gain, arrived.at[1]),
    ]
    for copy in copies:
        copy.start()
    for copy in copies:
        copy.wait()
    gain_rows = jnp.broadcast_to(gain[...].astype(F32), (8, LANES))
    block = jnp.concatenate([tokens[...].astype(F32), gain_rows], axis=0).astype(BF16)
    for target in range(out.shape[0]):
        out[target] = block


def early_kernel(
    place,
    stretch,
    cache,
    slot,
    wanted,
    down_hbm,
    numbers,
    ranges,
    places,
    down,
    arrived,
):
    copy = pltpu.make_async_copy(down_hbm, down, arrived)
    copy.start()
    numbers[...] = jnp.zeros(numbers.shape, jnp.int32)
    for row, part in ((SLOT_ROW, slot), (WANTED_ROW, wanted)):
        numbers[row : row + 1, : part.shape[1]] = part[...]
    parts = place.shape[0]
    for part in range(parts):
        places[part * LANES : (part + 1) * LANES, :] = column_of(place[part : part + 1, :])

    def wide(row):
        return jnp.broadcast_to(row.astype(F32), (LANES, LANES))

    cache_row = jnp.concatenate(
        [cache[...], jnp.zeros((1, LANES - cache.shape[1]), jnp.int32)], axis=1
    )
    uppers = [cache_row] + [stretch[part : part + 1, :] for part in range(parts)]
    counts = [jnp.zeros((1, LANES), F32) for _ in range(1 + len(uppers))]
    for part in range(parts):
        column = column_of(stretch[part : part + 1, :])
        below = jnp.where(column < wide(cache_row), 1.0, 0.0)
        counts[0] = counts[0] + jnp.sum(below, axis=0, keepdims=True)
        for index, row in enumerate(uppers):
            below = jnp.where(column <= wide(row), 1.0, 0.0)
            counts[1 + index] = counts[1 + index] + jnp.sum(below, axis=0, keepdims=True)
    counts.append(jnp.zeros((8 - len(counts), LANES), F32))
    ranges[...] = jnp.concatenate(counts, axis=0).astype(jnp.int32)
    copy.wait()


def adapter_choice(numbers, place, first_home):
    use_first = jnp.zeros(place.shape, jnp.bool_)
    use_second = jnp.zeros(place.shape, jnp.bool_)
    for wanted_index in range(NEED):
        home = home_of(numbers, wanted_index)
        here = place == float(wanted_index)
        use_first = use_first | (here & (home == first_home))
        use_second = use_second | (here & (home == first_home + 1))
    return use_first, use_second


def middle_kernel(numbers, places, blocks, down, out, flat):
    rows = flat.shape[0]
    squares = jnp.zeros((rows, LANES), F32)
    for source in range(blocks.shape[0]):
        block = blocks[source].astype(F32)
        token_part = block[:rows]
        squares = squares + token_part * token_part
        scaled = (token_part * block[rows : rows + 1]).astype(BF16)
        flat[:, source * LANES : (source + 1) * LANES] = scaled
    mean = jnp.sum(squares, axis=1, keepdims=True) / MODEL_WIDTH
    inverse = lax.rsqrt(mean + EPSILON)
    middle = contract_last(flat[...], down[...]) * inverse
    first = pl.multiple_of(lax.axis_index("head") * rows, rows)
    use_first, use_second = adapter_choice(
        numbers, places[pl.ds(first, rows), :], lax.axis_index("ctx") * 2
    )
    picked = jnp.where(
        use_first, middle, jnp.where(use_second, pltpu.roll(middle, RANK, 1), 0.0)
    )
    picked = picked.astype(BF16).astype(F32)
    packed = jnp.where(
        lane_iota((rows, LANES)) < RANK, picked, jnp.broadcast_to(inverse, (rows, LANES))
    )
    for target in range(out.shape[0]):
        out[target] = packed


def project_kernel(
    numbers, places, tokens, gain, middles, query_matrix, key_matrix, value_matrix, up, out
):
    scaled = (tokens[...].astype(F32) * gain[...].astype(F32)).astype(BF16)
    packed = middles[...]
    lanes = lane_iota(packed.shape)
    inverse = packed[:, RANK : RANK + 1]
    use_first, use_second = adapter_choice(numbers, places[...], lax.axis_index("ctx") * 2)
    spread = jnp.where(
        lanes < RANK,
        jnp.where(use_first, packed, 0.0),
        jnp.where(use_second, pltpu.roll(packed, RANK, 1), 0.0),
    ).astype(BF16)
    columns = up.shape[1]
    change = jnp.dot(spread, up[...], preferred_element_type=F32)
    query = jnp.dot(scaled, query_matrix[...], preferred_element_type=F32)
    out[:, :columns] = (query * inverse + ADAPTER_SCALE * change).astype(BF16)
    key = jnp.dot(scaled, key_matrix[...], preferred_element_type=F32)
    out[:, columns : columns + HEAD_WIDTH] = (key * inverse).astype(BF16)
    value = jnp.dot(scaled, value_matrix[...], preferred_element_type=F32)
    out[:, columns + HEAD_WIDTH :] = (value * inverse).astype(BF16)


def sum_kernel(parts, out, own_pair):
    total = parts[0].astype(F32)
    for source in range(1, parts.shape[0]):
        total = total + parts[source].astype(F32)
    query_columns = out.shape[2]
    queries = total[:, :query_columns].astype(BF16)
    for target in range(out.shape[0]):
        out[target] = queries
    own_pair[...] = total[:, query_columns:]


def attention_kernel(
    ranges,
    vectors,
    own_pair,
    keys,
    values,
    out,
    queries,
    peaks,
    masses,
    sums,
    scores,
):
    sources, own_rows, _ = vectors.shape
    total_rows = sources * own_rows
    block_count = keys.shape[0] // SPAN
    head_columns = GROUP * HEAD_WIDTH
    tall = GROUP * WINDOW
    window_row = row_iota((tall, LANES))
    window_row = window_row - WINDOW * (window_row // WINDOW)
    peaks[...] = jnp.full(peaks.shape, LOWEST, F32)
    masses[...] = jnp.zeros(masses.shape, F32)
    sums[...] = jnp.zeros(sums.shape, F32)

    lanes = lane_iota((total_rows, LANES))
    for g in range(GROUP):
        for source in range(sources):
            queries[g, source * own_rows : (source + 1) * own_rows, :] = vectors[
                source, :, g * HEAD_WIDTH : (g + 1) * HEAD_WIDTH
            ].astype(F32)

    def window_of(block):
        begin = ranges[0, block]
        start = jnp.minimum((begin // 8) * 8, total_rows - WINDOW)
        return pl.multiple_of(start, 8), begin, ranges[1, block]

    def load(ref, start):
        return jnp.concatenate([ref[g, pl.ds(start, WINDOW), :] for g in range(GROUP)], axis=0)

    def raise_peaks(start, result):
        for g in range(GROUP):
            place = pl.ds(start, WINDOW)
            peaks[g, place, :] = jnp.maximum(
                peaks[g, place, :], result[g * WINDOW : (g + 1) * WINDOW]
            )

    def add_up(start, weights, product):
        for g in range(GROUP):
            place = pl.ds(start, WINDOW)
            rows = slice(g * WINDOW, (g + 1) * WINDOW)
            masses[g, place, :] = masses[g, place, :] + weights[rows]
            sums[g, place, :] = sums[g, place, :] + product[rows]

    own_first = pl.multiple_of(lax.axis_index("ctx") * own_rows, own_rows)
    padding = jnp.zeros((LANES - own_rows, HEAD_WIDTH), F32)
    new_keys = jnp.concatenate([own_pair[:, :HEAD_WIDTH], padding], axis=0).astype(BF16)
    new_values = jnp.concatenate([own_pair[:, HEAD_WIDTH:], padding], axis=0).astype(BF16)
    own_start = pl.multiple_of(jnp.minimum(own_first, total_rows - WINDOW), 8)
    key_lane = lane_iota((tall, LANES))
    ends = jnp.zeros((tall, LANES), jnp.int32)
    for j in range(own_rows):
        position = own_first + j
        ends = jnp.where(key_lane == j, ranges[2 + position // LANES, position % LANES], ends)
    query_position = window_row + own_start
    allowed = (key_lane + own_first <= query_position) & (query_position < ends)
    own_scores = contract_last(load(queries, own_start).astype(BF16), new_keys)
    own_scores = jnp.where(allowed, own_scores * SCORE_SCALE, LOWEST)
    raise_peaks(own_start, own_scores)

    unroll = 32

    def score_step(step, carry):
        found = []
        for k in range(unroll):
            block = step * unroll + k
            start, begin, end = window_of(block)
            key_block = keys[pl.ds(pl.multiple_of(block * SPAN, SPAN), SPAN), :]
            result = contract_last(load(queries, start).astype(BF16), key_block)
            position = window_row + start
            allowed = (position >= begin) & (position < end)
            result = jnp.where(allowed, result * SCORE_SCALE, LOWEST)
            scores[block] = result
            found.append((start, result))
        for start, result in found:
            raise_peaks(start, result)
        return carry

    lax.fori_loop(0, block_count // unroll, score_step, 0)
    for g in range(GROUP):
        highest = jnp.max(peaks[g], axis=1, keepdims=True)
        peaks[g] = jnp.broadcast_to(jnp.maximum(highest, FLOOR), (total_rows, LANES))

    own_weights = jnp.exp2(own_scores - load(peaks, own_start))
    add_up(
        own_start,
        own_weights,
        jnp.dot(own_weights.astype(BF16), new_values, preferred_element_type=F32),
    )

    def value_step(step, carry):
        found = []
        for k in range(unroll):
            block = step * unroll + k
            start, begin, end = window_of(block)
            weights = jnp.exp2(scores[block] - load(peaks, start))
            value_block = values[pl.ds(pl.multiple_of(block * SPAN, SPAN), SPAN), :]
            product = jnp.dot(weights.astype(BF16), value_block, preferred_element_type=F32)
            found.append((start, weights, product))
        for start, weights, product in found:
            add_up(start, weights, product)
        return carry

    lax.fori_loop(0, block_count // unroll, value_step, 0)

    quarter = lanes % GROUP
    peak_all = jnp.zeros((total_rows, LANES), F32)
    mass_all = jnp.zeros((total_rows, LANES), F32)
    for g in range(GROUP):
        mass = jnp.sum(masses[g], axis=1, keepdims=True)
        scale = jnp.where(mass > 0.0, 1.0 / mass, 0.0)
        out[:, g * HEAD_WIDTH : (g + 1) * HEAD_WIDTH] = (sums[g] * scale).astype(BF16)
        peak_all = jnp.where(quarter == g, peaks[g], peak_all)
        mass_all = jnp.where(quarter == g, mass, mass_all)
    notes = jnp.zeros((total_rows, LANES), F32)
    for index, part in enumerate(thirds(peak_all) + thirds(mass_all)):
        inside = (lanes >= GROUP * index) & (lanes < GROUP * (index + 1))
        notes = jnp.where(inside, part, notes)
    out[:, head_columns:] = notes.astype(BF16)


def combine_kernel(parts, out):
    sources, own_rows, _ = parts.shape
    head_columns = GROUP * HEAD_WIDTH
    peaks = []
    masses = []
    for source in range(sources):
        notes = parts[source, :, head_columns:].astype(F32)

        def from_lane(index):
            if index == 0:
                return notes
            return pltpu.roll(notes, LANES - GROUP * index, 1)

        peaks.append(from_lane(0) + from_lane(1) + from_lane(2))
        masses.append(from_lane(3) + from_lane(4) + from_lane(5))
    highest = peaks[0]
    for source in range(1, sources):
        highest = jnp.maximum(highest, peaks[source])
    weights = [masses[s] * jnp.exp2(peaks[s] - highest) for s in range(sources)]
    total = weights[0]
    for source in range(1, sources):
        total = total + weights[source]
    results = [jnp.zeros((own_rows, HEAD_WIDTH), F32) for _ in range(GROUP)]
    for source in range(sources):
        share = weights[source] / total
        for g in range(GROUP):
            part = parts[source, :, g * HEAD_WIDTH : (g + 1) * HEAD_WIDTH].astype(F32)
            results[g] = results[g] + share[:, g : g + 1] * part
    block = jnp.concatenate(results, axis=1).astype(BF16)
    for target in range(out.shape[0]):
        out[target] = block


def shards(
    tokens,
    input_norm_gain,
    query_matrix,
    key_matrix,
    value_matrix,
    output_matrix,
    cached_key_rows,
    cached_value_rows,
    cache_block_recording,
    stretch_token_recording,
    adapter_down_store,
    adapter_up_store,
    adapter_store_slot,
    adapter_wanted_list,
    token_adapter_place,
):
    total_rows = tokens.shape[0]
    ctx_count = lax.axis_size("ctx")
    head_count = lax.axis_size("head")
    own_rows = total_rows // ctx_count
    head_rows = total_rows // head_count
    query_columns = query_matrix.shape[1]
    block_count = cached_key_rows.shape[0] // SPAN
    down = adapter_down_store.reshape(2 * RANK, MODEL_WIDTH)
    up = adapter_up_store.reshape(2 * RANK, query_columns)

    place = token_adapter_place.reshape(total_rows // LANES, LANES)
    stretch = stretch_token_recording.reshape(total_rows // LANES, LANES)
    cache = cache_block_recording.reshape(1, block_count)
    slot = adapter_store_slot.reshape(1, adapter_store_slot.shape[0])
    wanted = adapter_wanted_list.reshape(1, NEED)
    gain = input_norm_gain.reshape(1, LANES)
    packed = call(
        pack_kernel,
        jax.ShapeDtypeStruct((ctx_count, head_rows + 8, LANES), BF16),
        [HBM, HBM],
        [
            pltpu.VMEM((head_rows, LANES), BF16),
            pltpu.VMEM((1, LANES), BF16),
            pltpu.SemaphoreType.DMA((2,)),
        ],
        limit=60,
        name="pack_tokens",
    )(tokens, gain)
    blocks = lax.all_to_all(packed, "ctx", 0, 0, tiled=True)
    all_columns = query_columns + 2 * HEAD_WIDTH
    numbers, ranges, places, down = call(
        early_kernel,
        (
            jax.ShapeDtypeStruct((8, LANES), jnp.int32),
            jax.ShapeDtypeStruct((8, LANES), jnp.int32),
            jax.ShapeDtypeStruct((total_rows, LANES), F32),
            jax.ShapeDtypeStruct(down.shape, BF16),
        ),
        [VMEM] * 5 + [HBM],
        [pltpu.SemaphoreType.DMA],
        name="early",
    )(place, stretch, cache, slot, wanted, down)
    middles = call(
        middle_kernel,
        jax.ShapeDtypeStruct((head_count, head_rows, LANES), F32),
        [SMEM] + [VMEM] * 3,
        [pltpu.VMEM((head_rows, MODEL_WIDTH), BF16)],
        name="adapter_middle",
    )(numbers, places, blocks, down)
    middles = lax.all_to_all(middles, "head", 0, 0, tiled=True).reshape(total_rows, LANES)
    partial = call(
        project_kernel,
        jax.ShapeDtypeStruct((total_rows, all_columns), BF16),
        [SMEM] + [VMEM] * 8,
        name="project",
    )(
        numbers,
        places,
        tokens,
        gain,
        middles,
        query_matrix,
        key_matrix,
        value_matrix,
        up,
    )
    partial = lax.all_to_all(
        partial.reshape(ctx_count, own_rows, all_columns), "ctx", 0, 0, tiled=True
    )
    vectors, own_pair = call(
        sum_kernel,
        (
            jax.ShapeDtypeStruct((ctx_count, own_rows, query_columns), BF16),
            jax.ShapeDtypeStruct((own_rows, 2 * HEAD_WIDTH), F32),
        ),
        [VMEM],
        name="sum_projections",
    )(partial)
    vectors = lax.all_to_all(vectors, "ctx", 0, 0, tiled=True)
    state = pltpu.VMEM((GROUP, total_rows, LANES), F32)
    parts = call(
        attention_kernel,
        jax.ShapeDtypeStruct((total_rows, query_columns + LANES), BF16),
        [SMEM] + [VMEM] * 4,
        [
            state,
            state,
            state,
            state,
            pltpu.VMEM((block_count, GROUP * WINDOW, LANES), F32),
        ],
        limit=24,
        name="attention",
    )(ranges, vectors, own_pair, cached_key_rows, cached_value_rows)
    parts = lax.all_to_all(
        parts.reshape(ctx_count, own_rows, query_columns + LANES), "ctx", 0, 0, tiled=True
    )
    attention = call(
        combine_kernel,
        jax.ShapeDtypeStruct((ctx_count, own_rows, query_columns), BF16),
        [VMEM],
        name="combine",
    )(parts)
    attention = lax.all_to_all(attention, "ctx", 0, 0, tiled=True).reshape(total_rows, query_columns)
    mixed = jnp.dot(attention, output_matrix, preferred_element_type=F32)
    mixed = lax.all_to_all(mixed.reshape(head_count, head_rows, LANES), "head", 0, 0, tiled=True)
    return jnp.sum(mixed, axis=0).astype(BF16)


def solution(mesh):
    in_specs = (
        P(None, "ctx"),
        P("ctx"),
        P("ctx", "head"),
        P("ctx", "head"),
        P("ctx", "head"),
        P("head", "ctx"),
        P("ctx", "head"),
        P("ctx", "head"),
        P("ctx"),
        P(),
        P("ctx", None, None),
        P("ctx", None, "head"),
        P(),
        P(),
        P(),
    )
    out_specs = P("head", "ctx")
    return jax.shard_map(shards, mesh=mesh, in_specs=in_specs, out_specs=out_specs, check_vma=False)
```

```python
import math

import jax
import jax.numpy as jnp
from jax import lax
from jax.experimental import pallas as pl
from jax.experimental.pallas import tpu as pltpu
from jax.sharding import PartitionSpec as P

MODEL_WIDTH = 4096
HEAD_WIDTH = 128
LANES = 128
SPAN = 128
NEED = 4
GROUP = 4
RANK = 64
WINDOW = 24

LOWEST = -1e30
FLOOR = -1e29
EPSILON = 1e-05
ADAPTER_SCALE = 0.5
SCORE_SCALE = math.log2(math.e) / math.sqrt(HEAD_WIDTH)

F32 = jnp.float32
BF16 = jnp.bfloat16
VMEM = pl.BlockSpec(memory_space=pltpu.VMEM)
SMEM = pl.BlockSpec(memory_space=pltpu.SMEM)
HBM = pl.BlockSpec(memory_space=pltpu.HBM)


def lane_iota(shape):
    return lax.broadcasted_iota(jnp.int32, shape, len(shape) - 1)


def row_iota(shape):
    return lax.broadcasted_iota(jnp.int32, shape, len(shape) - 2)


def column_of(row):
    return jnp.transpose(jnp.broadcast_to(row.astype(F32), (LANES, LANES)))


def thirds(value):
    high = value.astype(BF16).astype(F32)
    rest = value - high
    middle = rest.astype(BF16).astype(F32)
    return high, middle, rest - middle


def contract_last(a, b):
    return lax.dot_general(a, b, (((1,), (1,)), ((), ())), preferred_element_type=F32)


def call(body, out_shape, in_specs, scratch=(), limit=16, name=None):
    many = isinstance(out_shape, (tuple, list))
    return pl.pallas_call(
        body,
        out_shape=out_shape,
        in_specs=in_specs,
        out_specs=[VMEM] * len(out_shape) if many else VMEM,
        scratch_shapes=list(scratch),
        compiler_params=pltpu.CompilerParams(vmem_limit_bytes=limit * 1024 * 1024),
        name=name,
    )


PLACE_ROW, STRETCH_ROW, CACHE_ROW, SLOT_ROW, WANTED_ROW = 0, 2, 4, 5, 6


def pack_kernel(
    tokens_hbm,
    gain_hbm,
    place_hbm,
    stretch_hbm,
    cache_hbm,
    slot_hbm,
    wanted_hbm,
    out,
    table,
    tokens,
    gain,
    place,
    stretch,
    cache,
    slot,
    wanted,
    arrived,
):
    rows = tokens.shape[0]
    first = pl.multiple_of(lax.axis_index("head") * rows, rows)
    pairs = (
        (tokens_hbm.at[pl.ds(first, rows), :], tokens),
        (gain_hbm, gain),
        (place_hbm, place),
        (stretch_hbm, stretch),
        (cache_hbm, cache),
        (slot_hbm, slot),
        (wanted_hbm, wanted),
    )
    copies = [
        pltpu.make_async_copy(source, target, arrived.at[index])
        for index, (source, target) in enumerate(pairs)
    ]
    for copy in copies:
        copy.start()
    for copy in copies[:2]:
        copy.wait()
    gain_rows = jnp.broadcast_to(gain[...].astype(F32), (8, LANES))
    block = jnp.concatenate([tokens[...].astype(F32), gain_rows], axis=0).astype(BF16)
    for target in range(out.shape[0]):
        out[target] = block
    for copy in copies[2:]:
        copy.wait()
    table[...] = jnp.zeros(table.shape, jnp.int32)
    table[PLACE_ROW : PLACE_ROW + 2, :] = place[...]
    table[STRETCH_ROW : STRETCH_ROW + 2, :] = stretch[...]
    for row, part in ((CACHE_ROW, cache), (SLOT_ROW, slot), (WANTED_ROW, wanted)):
        table[row : row + 1, : part.shape[1]] = part[...]


def early_kernel(numbers, table, down_hbm, ranges, uses_first, uses_second, down, arrived):
    copy = pltpu.make_async_copy(down_hbm, down, arrived)
    copy.start()
    parts = uses_first.shape[0] // LANES
    first_home = lax.axis_index("ctx") * 2
    for part in range(parts):
        place = column_of(table[PLACE_ROW + part : PLACE_ROW + part + 1, :])
        rows = slice(part * LANES, (part + 1) * LANES)
        for stored, target in enumerate((uses_first, uses_second)):
            used = jnp.zeros(place.shape, F32)
            for wanted_index in range(NEED):
                match = numbers[SLOT_ROW, numbers[WANTED_ROW, wanted_index]] == first_home + stored
                used = jnp.where((place == float(wanted_index)) & match, 1.0, used)
            target[rows, :] = used

    def wide(row):
        return jnp.broadcast_to(table[row : row + 1, :].astype(F32), (LANES, LANES))

    counts = [jnp.zeros((1, LANES), F32) for _ in range(2 + parts)]
    for part in range(parts):
        row = STRETCH_ROW + part
        column = column_of(table[row : row + 1, :])
        below = jnp.where(column < wide(CACHE_ROW), 1.0, 0.0)
        counts[0] = counts[0] + jnp.sum(below, axis=0, keepdims=True)
        for index, upper in enumerate([CACHE_ROW] + [STRETCH_ROW + k for k in range(parts)]):
            below = jnp.where(column <= wide(upper), 1.0, 0.0)
            counts[1 + index] = counts[1 + index] + jnp.sum(below, axis=0, keepdims=True)
    counts.append(jnp.zeros((8 - len(counts), LANES), F32))
    ranges[...] = jnp.concatenate(counts, axis=0).astype(jnp.int32)
    copy.wait()


def middle_kernel(uses_first, uses_second, blocks, down, out, flat):
    rows = flat.shape[0]
    squares = jnp.zeros((rows, LANES), F32)
    for source in range(blocks.shape[0]):
        block = blocks[source].astype(F32)
        token_part = block[:rows]
        squares = squares + token_part * token_part
        scaled = (token_part * block[rows : rows + 1]).astype(BF16)
        flat[:, source * LANES : (source + 1) * LANES] = scaled
    mean = jnp.sum(squares, axis=1, keepdims=True) / MODEL_WIDTH
    inverse = lax.rsqrt(mean + EPSILON)
    middle = contract_last(flat[...], down[...]) * inverse
    first = pl.multiple_of(lax.axis_index("head") * rows, rows)
    picked = middle * uses_first[pl.ds(first, rows), :]
    picked = picked + pltpu.roll(middle, RANK, 1) * uses_second[pl.ds(first, rows), :]
    lanes = lane_iota((rows, LANES))
    high, mid, low = thirds(jnp.broadcast_to(inverse, (rows, LANES)))
    tail = jnp.where(
        lanes == RANK, high, jnp.where(lanes == RANK + 1, mid, jnp.where(lanes == RANK + 2, low, 0.0))
    )
    packed = jnp.where(lanes < RANK, picked, tail).astype(BF16)
    for target in range(out.shape[0]):
        out[target] = packed


def project_kernel(
    uses_first,
    uses_second,
    tokens,
    gain,
    middles,
    query_matrix,
    key_matrix,
    value_matrix,
    up,
    out,
):
    scaled = (tokens[...].astype(F32) * gain[...].astype(F32)).astype(BF16)
    packed = middles[...].astype(F32)
    lanes = lane_iota(packed.shape)
    inverse = jnp.sum(
        jnp.where((lanes >= RANK) & (lanes < RANK + 3), packed, 0.0), axis=1, keepdims=True
    )
    spread = jnp.where(
        lanes < RANK, packed * uses_first[...], pltpu.roll(packed, RANK, 1) * uses_second[...]
    ).astype(BF16)
    columns = up.shape[1]
    change = jnp.dot(spread, up[...], preferred_element_type=F32)
    query = jnp.dot(scaled, query_matrix[...], preferred_element_type=F32)
    out[:, :columns] = (query * inverse + ADAPTER_SCALE * change).astype(BF16)
    key = jnp.dot(scaled, key_matrix[...], preferred_element_type=F32)
    out[:, columns : columns + HEAD_WIDTH] = (key * inverse).astype(BF16)
    value = jnp.dot(scaled, value_matrix[...], preferred_element_type=F32)
    out[:, columns + HEAD_WIDTH :] = (value * inverse).astype(BF16)


def sum_kernel(parts, out, own_pair):
    total = parts[0].astype(F32)
    for source in range(1, parts.shape[0]):
        total = total + parts[source].astype(F32)
    query_columns = out.shape[2]
    queries = total[:, :query_columns].astype(BF16)
    for target in range(out.shape[0]):
        out[target] = queries
    own_pair[...] = total[:, query_columns:]


def attention_kernel(
    ranges,
    vectors,
    own_pair,
    keys,
    values,
    out,
    queries,
    peaks,
    masses,
    sums,
    scores,
):
    sources, own_rows, _ = vectors.shape
    total_rows = sources * own_rows
    block_count = keys.shape[0] // SPAN
    head_columns = GROUP * HEAD_WIDTH
    tall = GROUP * WINDOW
    window_row = row_iota((tall, LANES))
    window_row = window_row - WINDOW * (window_row // WINDOW)
    peaks[...] = jnp.full(peaks.shape, LOWEST, F32)
    masses[...] = jnp.zeros(masses.shape, F32)
    sums[...] = jnp.zeros(sums.shape, F32)

    lanes = lane_iota((total_rows, LANES))
    for g in range(GROUP):
        for source in range(sources):
            queries[g, source * own_rows : (source + 1) * own_rows, :] = vectors[
                source, :, g * HEAD_WIDTH : (g + 1) * HEAD_WIDTH
            ].astype(F32)

    def window_of(block):
        begin = ranges[0, block]
        start = jnp.minimum((begin // 8) * 8, total_rows - WINDOW)
        return pl.multiple_of(start, 8), begin, ranges[1, block]

    def load(ref, start):
        return jnp.concatenate([ref[g, pl.ds(start, WINDOW), :] for g in range(GROUP)], axis=0)

    def raise_peaks(start, result):
        for g in range(GROUP):
            place = pl.ds(start, WINDOW)
            peaks[g, place, :] = jnp.maximum(
                peaks[g, place, :], result[g * WINDOW : (g + 1) * WINDOW]
            )

    def add_up(start, weights, product):
        for g in range(GROUP):
            place = pl.ds(start, WINDOW)
            rows = slice(g * WINDOW, (g + 1) * WINDOW)
            masses[g, place, :] = masses[g, place, :] + weights[rows]
            sums[g, place, :] = sums[g, place, :] + product[rows]

    own_first = pl.multiple_of(lax.axis_index("ctx") * own_rows, own_rows)
    padding = jnp.zeros((LANES - own_rows, HEAD_WIDTH), F32)
    new_keys = jnp.concatenate([own_pair[:, :HEAD_WIDTH], padding], axis=0).astype(BF16)
    new_values = jnp.concatenate([own_pair[:, HEAD_WIDTH:], padding], axis=0).astype(BF16)
    own_start = pl.multiple_of(jnp.minimum(own_first, total_rows - WINDOW), 8)
    key_lane = lane_iota((tall, LANES))
    ends = jnp.zeros((tall, LANES), jnp.int32)
    for j in range(own_rows):
        position = own_first + j
        ends = jnp.where(key_lane == j, ranges[2 + position // LANES, position % LANES], ends)
    query_position = window_row + own_start
    allowed = (key_lane + own_first <= query_position) & (query_position < ends)
    own_scores = contract_last(load(queries, own_start).astype(BF16), new_keys)
    own_scores = jnp.where(allowed, own_scores * SCORE_SCALE, LOWEST)
    raise_peaks(own_start, own_scores)

    unroll = 64

    def score_step(step, carry):
        found = []
        for k in range(unroll):
            block = step * unroll + k
            start, begin, end = window_of(block)
            key_block = keys[pl.ds(pl.multiple_of(block * SPAN, SPAN), SPAN), :]
            result = contract_last(load(queries, start).astype(BF16), key_block)
            allowed = (window_row >= begin - start) & (window_row < end - start)
            result = jnp.where(allowed, result * SCORE_SCALE, LOWEST)
            scores[block] = result
            found.append((start, result))
        for start, result in found:
            raise_peaks(start, result)
        return carry

    lax.fori_loop(0, block_count // unroll, score_step, 0)
    for g in range(GROUP):
        highest = jnp.max(peaks[g], axis=1, keepdims=True)
        peaks[g] = jnp.broadcast_to(jnp.maximum(highest, FLOOR), (total_rows, LANES))

    own_weights = jnp.exp2(own_scores - load(peaks, own_start))
    add_up(
        own_start,
        own_weights,
        jnp.dot(own_weights.astype(BF16), new_values, preferred_element_type=F32),
    )

    def value_step(step, carry):
        found = []
        for k in range(unroll):
            block = step * unroll + k
            start, begin, end = window_of(block)
            weights = jnp.exp2(scores[block] - load(peaks, start))
            value_block = values[pl.ds(pl.multiple_of(block * SPAN, SPAN), SPAN), :]
            product = jnp.dot(weights.astype(BF16), value_block, preferred_element_type=F32)
            found.append((start, weights, product))
        for start, weights, product in found:
            add_up(start, weights, product)
        return carry

    lax.fori_loop(0, block_count // unroll, value_step, 0)

    quarter = lanes % GROUP
    peak_all = jnp.zeros((total_rows, LANES), F32)
    mass_all = jnp.zeros((total_rows, LANES), F32)
    for g in range(GROUP):
        mass = jnp.sum(masses[g], axis=1, keepdims=True)
        scale = jnp.where(mass > 0.0, 1.0 / mass, 0.0)
        out[:, g * HEAD_WIDTH : (g + 1) * HEAD_WIDTH] = (sums[g] * scale).astype(BF16)
        peak_all = jnp.where(quarter == g, peaks[g], peak_all)
        mass_all = jnp.where(quarter == g, mass, mass_all)
    notes = jnp.zeros((total_rows, LANES), F32)
    for index, part in enumerate(thirds(peak_all) + thirds(mass_all)):
        inside = (lanes >= GROUP * index) & (lanes < GROUP * (index + 1))
        notes = jnp.where(inside, part, notes)
    out[:, head_columns:] = notes.astype(BF16)


def combine_kernel(parts, out):
    sources, own_rows, _ = parts.shape
    head_columns = GROUP * HEAD_WIDTH
    peaks = []
    masses = []
    for source in range(sources):
        notes = parts[source, :, head_columns:].astype(F32)

        def from_lane(index):
            if index == 0:
                return notes
            return pltpu.roll(notes, LANES - GROUP * index, 1)

        peaks.append(from_lane(0) + from_lane(1) + from_lane(2))
        masses.append(from_lane(3) + from_lane(4) + from_lane(5))
    highest = peaks[0]
    for source in range(1, sources):
        highest = jnp.maximum(highest, peaks[source])
    weights = [masses[s] * jnp.exp2(peaks[s] - highest) for s in range(sources)]
    total = weights[0]
    for source in range(1, sources):
        total = total + weights[source]
    results = [jnp.zeros((own_rows, HEAD_WIDTH), F32) for _ in range(GROUP)]
    for source in range(sources):
        share = weights[source] / total
        for g in range(GROUP):
            part = parts[source, :, g * HEAD_WIDTH : (g + 1) * HEAD_WIDTH].astype(F32)
            results[g] = results[g] + share[:, g : g + 1] * part
    block = jnp.concatenate(results, axis=1).astype(BF16)
    for target in range(out.shape[0]):
        out[target] = block


def shards(
    tokens,
    input_norm_gain,
    query_matrix,
    key_matrix,
    value_matrix,
    output_matrix,
    cached_key_rows,
    cached_value_rows,
    cache_block_recording,
    stretch_token_recording,
    adapter_down_store,
    adapter_up_store,
    adapter_store_slot,
    adapter_wanted_list,
    token_adapter_place,
):
    total_rows = tokens.shape[0]
    ctx_count = lax.axis_size("ctx")
    head_count = lax.axis_size("head")
    own_rows = total_rows // ctx_count
    head_rows = total_rows // head_count
    query_columns = query_matrix.shape[1]
    block_count = cached_key_rows.shape[0] // SPAN
    down = adapter_down_store.reshape(2 * RANK, MODEL_WIDTH)
    up = adapter_up_store.reshape(2 * RANK, query_columns)

    place = token_adapter_place.reshape(total_rows // LANES, LANES)
    stretch = stretch_token_recording.reshape(total_rows // LANES, LANES)
    cache = cache_block_recording.reshape(1, block_count)
    slot = adapter_store_slot.reshape(1, adapter_store_slot.shape[0])
    wanted = adapter_wanted_list.reshape(1, NEED)
    gain = input_norm_gain.reshape(1, LANES)
    packed, table = call(
        pack_kernel,
        (
            jax.ShapeDtypeStruct((ctx_count, head_rows + 8, LANES), BF16),
            jax.ShapeDtypeStruct((8, LANES), jnp.int32),
        ),
        [HBM] * 7,
        [
            pltpu.VMEM((head_rows, LANES), BF16),
            pltpu.VMEM((1, LANES), BF16),
            pltpu.VMEM(place.shape, jnp.int32),
            pltpu.VMEM(stretch.shape, jnp.int32),
            pltpu.VMEM(cache.shape, jnp.int32),
            pltpu.VMEM(slot.shape, jnp.int32),
            pltpu.VMEM(wanted.shape, jnp.int32),
            pltpu.SemaphoreType.DMA((7,)),
        ],
        limit=60,
        name="pack_tokens",
    )(tokens, gain, place, stretch, cache, slot, wanted)
    blocks = lax.all_to_all(packed, "ctx", 0, 0, tiled=True)
    all_columns = query_columns + 2 * HEAD_WIDTH
    mask = jax.ShapeDtypeStruct((total_rows, LANES), F32)
    ranges, uses_first, uses_second, down = call(
        early_kernel,
        (
            jax.ShapeDtypeStruct((8, LANES), jnp.int32),
            mask,
            mask,
            jax.ShapeDtypeStruct(down.shape, BF16),
        ),
        [SMEM, VMEM, HBM],
        [pltpu.SemaphoreType.DMA],
        name="early",
    )(table, table, down)
    middles = call(
        middle_kernel,
        jax.ShapeDtypeStruct((head_count, head_rows, LANES), BF16),
        [VMEM] * 4,
        [pltpu.VMEM((head_rows, MODEL_WIDTH), BF16)],
        name="adapter_middle",
    )(uses_first, uses_second, blocks, down)
    middles = lax.all_to_all(middles, "head", 0, 0, tiled=True).reshape(total_rows, LANES)
    partial = call(
        project_kernel,
        jax.ShapeDtypeStruct((total_rows, all_columns), BF16),
        [VMEM] * 9,
        name="project",
    )(
        uses_first,
        uses_second,
        tokens,
        gain,
        middles,
        query_matrix,
        key_matrix,
        value_matrix,
        up,
    )
    partial = lax.all_to_all(
        partial.reshape(ctx_count, own_rows, all_columns), "ctx", 0, 0, tiled=True
    )
    vectors, own_pair = call(
        sum_kernel,
        (
            jax.ShapeDtypeStruct((ctx_count, own_rows, query_columns), BF16),
            jax.ShapeDtypeStruct((own_rows, 2 * HEAD_WIDTH), F32),
        ),
        [VMEM],
        name="sum_projections",
    )(partial)
    vectors = lax.all_to_all(vectors, "ctx", 0, 0, tiled=True)
    state = pltpu.VMEM((GROUP, total_rows, LANES), F32)
    parts = call(
        attention_kernel,
        jax.ShapeDtypeStruct((total_rows, query_columns + LANES), BF16),
        [SMEM] + [VMEM] * 4,
        [
            state,
            state,
            state,
            state,
            pltpu.VMEM((block_count, GROUP * WINDOW, LANES), F32),
        ],
        limit=24,
        name="attention",
    )(ranges, vectors, own_pair, cached_key_rows, cached_value_rows)
    parts = lax.all_to_all(
        parts.reshape(ctx_count, own_rows, query_columns + LANES), "ctx", 0, 0, tiled=True
    )
    attention = call(
        combine_kernel,
        jax.ShapeDtypeStruct((ctx_count, own_rows, query_columns), BF16),
        [VMEM],
        name="combine",
    )(parts)
    attention = lax.all_to_all(attention, "ctx", 0, 0, tiled=True).reshape(total_rows, query_columns)
    mixed = jnp.dot(attention, output_matrix, preferred_element_type=F32)
    mixed = mixed.astype(BF16).reshape(head_count, head_rows, LANES)
    mixed = lax.all_to_all(mixed, "head", 0, 0, tiled=True)
    return jnp.sum(mixed.astype(F32), axis=0).astype(BF16)


def solution(mesh):
    in_specs = (
        P(None, "ctx"),
        P("ctx"),
        P("ctx", "head"),
        P("ctx", "head"),
        P("ctx", "head"),
        P("head", "ctx"),
        P("ctx", "head"),
        P("ctx", "head"),
        P("ctx"),
        P(),
        P("ctx", None, None),
        P("ctx", None, "head"),
        P(),
        P(),
        P(),
    )
    out_specs = P("head", "ctx")
    return jax.shard_map(shards, mesh=mesh, in_specs=in_specs, out_specs=out_specs, check_vma=False)
```

```python
import math

import jax
import jax.numpy as jnp
from jax import lax
from jax.experimental import pallas as pl
from jax.experimental.pallas import tpu as pltpu
from jax.sharding import PartitionSpec as P

MODEL_WIDTH = 4096
HEAD_WIDTH = 128
LANES = 128
SPAN = 128
NEED = 4
GROUP = 4
RANK = 64
WINDOW = 24
BATCH = 16

LOWEST = -1e30
FLOOR = -1e29
EPSILON = 1e-05
ADAPTER_SCALE = 0.5
SCORE_SCALE = math.log2(math.e) / math.sqrt(HEAD_WIDTH)

F32 = jnp.float32
BF16 = jnp.bfloat16
VMEM = pl.BlockSpec(memory_space=pltpu.VMEM)
SMEM = pl.BlockSpec(memory_space=pltpu.SMEM)
HBM = pl.BlockSpec(memory_space=pltpu.HBM)


def lane_iota(shape):
    return lax.broadcasted_iota(jnp.int32, shape, len(shape) - 1)


def row_iota(shape):
    return lax.broadcasted_iota(jnp.int32, shape, len(shape) - 2)


def column_of(row):
    return jnp.transpose(jnp.broadcast_to(row.astype(F32), (LANES, LANES)))


def thirds(value):
    high = value.astype(BF16).astype(F32)
    rest = value - high
    middle = rest.astype(BF16).astype(F32)
    return high, middle, rest - middle


def contract_last(a, b):
    return lax.dot_general(a, b, (((1,), (1,)), ((), ())), preferred_element_type=F32)


def call(body, out_shape, in_specs, scratch=(), limit=16, name=None, out_specs=None):
    many = isinstance(out_shape, (tuple, list))
    return pl.pallas_call(
        body,
        out_shape=out_shape,
        in_specs=in_specs,
        out_specs=out_specs or ([VMEM] * len(out_shape) if many else VMEM),
        scratch_shapes=list(scratch),
        compiler_params=pltpu.CompilerParams(vmem_limit_bytes=limit * 1024 * 1024),
        name=name,
    )


PLACE_ROW, STRETCH_ROW, CACHE_ROW, SLOT_ROW, WANTED_ROW = 0, 2, 4, 5, 6


def pack_kernel(
    tokens_hbm,
    gain_hbm,
    place_hbm,
    stretch_hbm,
    cache_hbm,
    slot_hbm,
    wanted_hbm,
    out_hbm,
    table,
    tokens,
    gain,
    place,
    stretch,
    cache,
    slot,
    wanted,
    blocks,
    arrived,
    sent,
):
    rows = tokens.shape[0]
    first = pl.multiple_of(lax.axis_index("head") * rows, rows)
    pairs = (
        (tokens_hbm.at[pl.ds(first, rows), :], tokens),
        (gain_hbm, gain),
        (place_hbm, place),
        (stretch_hbm, stretch),
        (cache_hbm, cache),
        (slot_hbm, slot),
        (wanted_hbm, wanted),
    )
    copies = [
        pltpu.make_async_copy(source, target, arrived.at[index])
        for index, (source, target) in enumerate(pairs)
    ]
    for copy in copies:
        copy.start()
    for copy in copies[:2]:
        copy.wait()
    gain_rows = jnp.broadcast_to(gain[...].astype(F32), (8, LANES))
    block = jnp.concatenate([tokens[...].astype(F32), gain_rows], axis=0).astype(BF16)
    batch = blocks.shape[0]
    for target in range(batch):
        blocks[target] = block
    sends = [
        pltpu.make_async_copy(blocks, out_hbm.at[pl.ds(index * batch, batch)], sent.at[index])
        for index in range(out_hbm.shape[0] // batch)
    ]
    for copy in sends:
        copy.start()
    for copy in copies[2:]:
        copy.wait()
    table[...] = jnp.zeros(table.shape, jnp.int32)
    table[PLACE_ROW : PLACE_ROW + 2, :] = place[...]
    table[STRETCH_ROW : STRETCH_ROW + 2, :] = stretch[...]
    for row, part in ((CACHE_ROW, cache), (SLOT_ROW, slot), (WANTED_ROW, wanted)):
        table[row : row + 1, : part.shape[1]] = part[...]
    for copy in sends:
        copy.wait()


def early_kernel(numbers, table, down_hbm, ranges, uses_first, uses_second, down, arrived):
    copy = pltpu.make_async_copy(down_hbm, down, arrived)
    copy.start()
    parts = uses_first.shape[0] // LANES
    first_home = lax.axis_index("ctx") * 2
    for part in range(parts):
        place = column_of(table[PLACE_ROW + part : PLACE_ROW + part + 1, :])
        rows = slice(part * LANES, (part + 1) * LANES)
        for stored, target in enumerate((uses_first, uses_second)):
            used = jnp.zeros(place.shape, F32)
            for wanted_index in range(NEED):
                match = numbers[SLOT_ROW, numbers[WANTED_ROW, wanted_index]] == first_home + stored
                used = jnp.where((place == float(wanted_index)) & match, 1.0, used)
            target[rows, :] = used

    def wide(row):
        return jnp.broadcast_to(table[row : row + 1, :].astype(F32), (LANES, LANES))

    counts = [jnp.zeros((1, LANES), F32) for _ in range(2 + parts)]
    for part in range(parts):
        row = STRETCH_ROW + part
        column = column_of(table[row : row + 1, :])
        below = jnp.where(column < wide(CACHE_ROW), 1.0, 0.0)
        counts[0] = counts[0] + jnp.sum(below, axis=0, keepdims=True)
        for index, upper in enumerate([CACHE_ROW] + [STRETCH_ROW + k for k in range(parts)]):
            below = jnp.where(column <= wide(upper), 1.0, 0.0)
            counts[1 + index] = counts[1 + index] + jnp.sum(below, axis=0, keepdims=True)
    counts.append(jnp.zeros((8 - len(counts), LANES), F32))
    ranges[...] = jnp.concatenate(counts, axis=0).astype(jnp.int32)
    copy.wait()


def middle_kernel(uses_first, uses_second, blocks, down, out, flat):
    rows = flat.shape[0]
    squares = jnp.zeros((rows, LANES), F32)
    for source in range(blocks.shape[0]):
        block = blocks[source].astype(F32)
        token_part = block[:rows]
        squares = squares + token_part * token_part
        scaled = (token_part * block[rows : rows + 1]).astype(BF16)
        flat[:, source * LANES : (source + 1) * LANES] = scaled
    mean = jnp.sum(squares, axis=1, keepdims=True) / MODEL_WIDTH
    inverse = lax.rsqrt(mean + EPSILON)
    middle = contract_last(flat[...], down[...]) * inverse
    first = pl.multiple_of(lax.axis_index("head") * rows, rows)
    picked = middle * uses_first[pl.ds(first, rows), :]
    picked = picked + pltpu.roll(middle, RANK, 1) * uses_second[pl.ds(first, rows), :]
    lanes = lane_iota((rows, LANES))
    high, mid, low = thirds(jnp.broadcast_to(inverse, (rows, LANES)))
    tail = jnp.where(
        lanes == RANK, high, jnp.where(lanes == RANK + 1, mid, jnp.where(lanes == RANK + 2, low, 0.0))
    )
    packed = jnp.where(lanes < RANK, picked, tail).astype(BF16)
    for target in range(out.shape[0]):
        out[target] = packed


def project_kernel(
    uses_first,
    uses_second,
    tokens,
    gain,
    middles,
    query_matrix,
    key_matrix,
    value_matrix,
    up,
    out,
):
    scaled = (tokens[...].astype(F32) * gain[...].astype(F32)).astype(BF16)
    packed = middles[...].astype(F32)
    lanes = lane_iota(packed.shape)
    inverse = jnp.sum(
        jnp.where((lanes >= RANK) & (lanes < RANK + 3), packed, 0.0), axis=1, keepdims=True
    )
    spread = jnp.where(
        lanes < RANK, packed * uses_first[...], pltpu.roll(packed, RANK, 1) * uses_second[...]
    ).astype(BF16)
    columns = up.shape[1]
    change = jnp.dot(spread, up[...], preferred_element_type=F32)
    query = jnp.dot(scaled, query_matrix[...], preferred_element_type=F32)
    out[:, :columns] = (query * inverse + ADAPTER_SCALE * change).astype(BF16)
    key = jnp.dot(scaled, key_matrix[...], preferred_element_type=F32)
    out[:, columns : columns + HEAD_WIDTH] = (key * inverse).astype(BF16)
    value = jnp.dot(scaled, value_matrix[...], preferred_element_type=F32)
    out[:, columns + HEAD_WIDTH :] = (value * inverse).astype(BF16)


def sum_kernel(parts, out, own_pair):
    total = parts[0].astype(F32)
    for source in range(1, parts.shape[0]):
        total = total + parts[source].astype(F32)
    query_columns = out.shape[2]
    queries = total[:, :query_columns].astype(BF16)
    for target in range(out.shape[0]):
        out[target] = queries
    own_pair[...] = total[:, query_columns:]


def attention_kernel(
    ranges,
    vectors,
    own_pair,
    keys,
    values,
    out,
    queries,
    peaks,
    masses,
    sums,
    scores,
):
    sources, own_rows, _ = vectors.shape
    total_rows = sources * own_rows
    block_count = keys.shape[0] // SPAN
    head_columns = GROUP * HEAD_WIDTH
    tall = GROUP * WINDOW
    window_row = row_iota((tall, LANES))
    window_row = window_row - WINDOW * (window_row // WINDOW)
    peaks[...] = jnp.full(peaks.shape, LOWEST, F32)
    masses[...] = jnp.zeros(masses.shape, F32)
    sums[...] = jnp.zeros(sums.shape, F32)

    lanes = lane_iota((total_rows, LANES))
    for g in range(GROUP):
        for source in range(sources):
            queries[g, source * own_rows : (source + 1) * own_rows, :] = vectors[
                source, :, g * HEAD_WIDTH : (g + 1) * HEAD_WIDTH
            ].astype(F32)

    def window_of(block):
        begin = ranges[0, block]
        start = jnp.minimum((begin // 8) * 8, total_rows - WINDOW)
        return pl.multiple_of(start, 8), begin, ranges[1, block]

    def load(ref, start):
        return jnp.concatenate([ref[g, pl.ds(start, WINDOW), :] for g in range(GROUP)], axis=0)

    def raise_peaks(start, result):
        for g in range(GROUP):
            place = pl.ds(start, WINDOW)
            peaks[g, place, :] = jnp.maximum(
                peaks[g, place, :], result[g * WINDOW : (g + 1) * WINDOW]
            )

    def add_up(start, weights, product):
        for g in range(GROUP):
            place = pl.ds(start, WINDOW)
            rows = slice(g * WINDOW, (g + 1) * WINDOW)
            masses[g, place, :] = masses[g, place, :] + weights[rows]
            sums[g, place, :] = sums[g, place, :] + product[rows]

    own_first = pl.multiple_of(lax.axis_index("ctx") * own_rows, own_rows)
    padding = jnp.zeros((LANES - own_rows, HEAD_WIDTH), F32)
    new_keys = jnp.concatenate([own_pair[:, :HEAD_WIDTH], padding], axis=0).astype(BF16)
    new_values = jnp.concatenate([own_pair[:, HEAD_WIDTH:], padding], axis=0).astype(BF16)
    own_start = pl.multiple_of(jnp.minimum(own_first, total_rows - WINDOW), 8)
    key_lane = lane_iota((tall, LANES))
    ends = jnp.zeros((tall, LANES), jnp.int32)
    for j in range(own_rows):
        position = own_first + j
        ends = jnp.where(key_lane == j, ranges[2 + position // LANES, position % LANES], ends)
    query_position = window_row + own_start
    allowed = (key_lane + own_first <= query_position) & (query_position < ends)
    own_scores = contract_last(load(queries, own_start).astype(BF16), new_keys)
    own_scores = jnp.where(allowed, own_scores * SCORE_SCALE, LOWEST)
    raise_peaks(own_start, own_scores)

    def score_blocks(first):
        found = []
        for block in range(first, first + BATCH):
            start, begin, end = window_of(block)
            key_block = keys[block * SPAN : (block + 1) * SPAN, :]
            result = contract_last(load(queries, start).astype(BF16), key_block)
            allowed = (window_row >= begin - start) & (window_row < end - start)
            result = jnp.where(allowed, result * SCORE_SCALE, LOWEST)
            scores[block] = result
            found.append((start, result))
        for start, result in found:
            raise_peaks(start, result)

    for first in range(0, block_count, BATCH):
        score_blocks(first)
    for g in range(GROUP):
        highest = jnp.max(peaks[g], axis=1, keepdims=True)
        peaks[g] = jnp.broadcast_to(jnp.maximum(highest, FLOOR), (total_rows, LANES))

    own_weights = jnp.exp2(own_scores - load(peaks, own_start))
    add_up(
        own_start,
        own_weights,
        jnp.dot(own_weights.astype(BF16), new_values, preferred_element_type=F32),
    )

    def value_blocks(first):
        found = []
        for block in range(first, first + BATCH):
            start, begin, end = window_of(block)
            weights = jnp.exp2(scores[block] - load(peaks, start))
            value_block = values[block * SPAN : (block + 1) * SPAN, :]
            product = jnp.dot(weights.astype(BF16), value_block, preferred_element_type=F32)
            found.append((start, weights, product))
        for start, weights, product in found:
            add_up(start, weights, product)

    for first in range(0, block_count, BATCH):
        value_blocks(first)

    quarter = lanes % GROUP
    peak_all = jnp.zeros((total_rows, LANES), F32)
    mass_all = jnp.zeros((total_rows, LANES), F32)
    for g in range(GROUP):
        mass = jnp.sum(masses[g], axis=1, keepdims=True)
        scale = jnp.where(mass > 0.0, 1.0 / mass, 0.0)
        out[:, g * HEAD_WIDTH : (g + 1) * HEAD_WIDTH] = (sums[g] * scale).astype(BF16)
        peak_all = jnp.where(quarter == g, peaks[g], peak_all)
        mass_all = jnp.where(quarter == g, mass, mass_all)
    notes = jnp.zeros((total_rows, LANES), F32)
    for index, part in enumerate(thirds(peak_all) + thirds(mass_all)):
        inside = (lanes >= GROUP * index) & (lanes < GROUP * (index + 1))
        notes = jnp.where(inside, part, notes)
    out[:, head_columns:] = notes.astype(BF16)


def combine_kernel(parts, out):
    sources, own_rows, _ = parts.shape
    head_columns = GROUP * HEAD_WIDTH
    peaks = []
    masses = []
    for source in range(sources):
        notes = parts[source, :, head_columns:].astype(F32)

        def from_lane(index):
            if index == 0:
                return notes
            return pltpu.roll(notes, LANES - GROUP * index, 1)

        peaks.append(from_lane(0) + from_lane(1) + from_lane(2))
        masses.append(from_lane(3) + from_lane(4) + from_lane(5))
    highest = peaks[0]
    for source in range(1, sources):
        highest = jnp.maximum(highest, peaks[source])
    weights = [masses[s] * jnp.exp2(peaks[s] - highest) for s in range(sources)]
    total = weights[0]
    for source in range(1, sources):
        total = total + weights[source]
    results = [jnp.zeros((own_rows, HEAD_WIDTH), F32) for _ in range(GROUP)]
    for source in range(sources):
        share = weights[source] / total
        for g in range(GROUP):
            part = parts[source, :, g * HEAD_WIDTH : (g + 1) * HEAD_WIDTH].astype(F32)
            results[g] = results[g] + share[:, g : g + 1] * part
    block = jnp.concatenate(results, axis=1).astype(BF16)
    for target in range(out.shape[0]):
        out[target] = block


def shards(
    tokens,
    input_norm_gain,
    query_matrix,
    key_matrix,
    value_matrix,
    output_matrix,
    cached_key_rows,
    cached_value_rows,
    cache_block_recording,
    stretch_token_recording,
    adapter_down_store,
    adapter_up_store,
    adapter_store_slot,
    adapter_wanted_list,
    token_adapter_place,
):
    total_rows = tokens.shape[0]
    ctx_count = lax.axis_size("ctx")
    head_count = lax.axis_size("head")
    own_rows = total_rows // ctx_count
    head_rows = total_rows // head_count
    query_columns = query_matrix.shape[1]
    block_count = cached_key_rows.shape[0] // SPAN
    down = adapter_down_store.reshape(2 * RANK, MODEL_WIDTH)
    up = adapter_up_store.reshape(2 * RANK, query_columns)

    place = token_adapter_place.reshape(total_rows // LANES, LANES)
    stretch = stretch_token_recording.reshape(total_rows // LANES, LANES)
    cache = cache_block_recording.reshape(1, block_count)
    slot = adapter_store_slot.reshape(1, adapter_store_slot.shape[0])
    wanted = adapter_wanted_list.reshape(1, NEED)
    gain = input_norm_gain.reshape(1, LANES)
    packed, table = call(
        pack_kernel,
        (
            jax.ShapeDtypeStruct((ctx_count, head_rows + 8, LANES), BF16),
            jax.ShapeDtypeStruct((8, LANES), jnp.int32),
        ),
        [HBM] * 7,
        [
            pltpu.VMEM((head_rows, LANES), BF16),
            pltpu.VMEM((1, LANES), BF16),
            pltpu.VMEM(place.shape, jnp.int32),
            pltpu.VMEM(stretch.shape, jnp.int32),
            pltpu.VMEM(cache.shape, jnp.int32),
            pltpu.VMEM(slot.shape, jnp.int32),
            pltpu.VMEM(wanted.shape, jnp.int32),
            pltpu.VMEM((8, head_rows + 8, LANES), BF16),
            pltpu.SemaphoreType.DMA((7,)),
            pltpu.SemaphoreType.DMA((ctx_count // 8,)),
        ],
        limit=60,
        name="pack_tokens",
        out_specs=[HBM, VMEM],
    )(tokens, gain, place, stretch, cache, slot, wanted)
    blocks = lax.all_to_all(packed, "ctx", 0, 0, tiled=True)
    all_columns = query_columns + 2 * HEAD_WIDTH
    mask = jax.ShapeDtypeStruct((total_rows, LANES), F32)
    ranges, uses_first, uses_second, down = call(
        early_kernel,
        (
            jax.ShapeDtypeStruct((8, LANES), jnp.int32),
            mask,
            mask,
            jax.ShapeDtypeStruct(down.shape, BF16),
        ),
        [SMEM, VMEM, HBM],
        [pltpu.SemaphoreType.DMA],
        name="early",
    )(table, table, down)
    middles = call(
        middle_kernel,
        jax.ShapeDtypeStruct((head_count, head_rows, LANES), BF16),
        [VMEM] * 4,
        [pltpu.VMEM((head_rows, MODEL_WIDTH), BF16)],
        name="adapter_middle",
    )(uses_first, uses_second, blocks, down)
    middles = lax.all_to_all(middles, "head", 0, 0, tiled=True).reshape(total_rows, LANES)
    partial = call(
        project_kernel,
        jax.ShapeDtypeStruct((total_rows, all_columns), BF16),
        [VMEM] * 9,
        name="project",
    )(
        uses_first,
        uses_second,
        tokens,
        gain,
        middles,
        query_matrix,
        key_matrix,
        value_matrix,
        up,
    )
    partial = lax.all_to_all(
        partial.reshape(ctx_count, own_rows, all_columns), "ctx", 0, 0, tiled=True
    )
    vectors, own_pair = call(
        sum_kernel,
        (
            jax.ShapeDtypeStruct((ctx_count, own_rows, query_columns), BF16),
            jax.ShapeDtypeStruct((own_rows, 2 * HEAD_WIDTH), F32),
        ),
        [VMEM],
        name="sum_projections",
    )(partial)
    vectors = lax.all_to_all(vectors, "ctx", 0, 0, tiled=True)
    state = pltpu.VMEM((GROUP, total_rows, LANES), F32)
    parts = call(
        attention_kernel,
        jax.ShapeDtypeStruct((total_rows, query_columns + LANES), BF16),
        [SMEM] + [VMEM] * 4,
        [
            state,
            state,
            state,
            state,
            pltpu.VMEM((block_count, GROUP * WINDOW, LANES), F32),
        ],
        limit=24,
        name="attention",
    )(ranges, vectors, own_pair, cached_key_rows, cached_value_rows)
    parts = lax.all_to_all(
        parts.reshape(ctx_count, own_rows, query_columns + LANES), "ctx", 0, 0, tiled=True
    )
    attention = call(
        combine_kernel,
        jax.ShapeDtypeStruct((ctx_count, own_rows, query_columns), BF16),
        [VMEM],
        name="combine",
    )(parts)
    attention = lax.all_to_all(attention, "ctx", 0, 0, tiled=True).reshape(total_rows, query_columns)
    mixed = jnp.dot(attention, output_matrix, preferred_element_type=F32)
    mixed = mixed.astype(BF16).reshape(head_count, head_rows, LANES)
    mixed = lax.all_to_all(mixed, "head", 0, 0, tiled=True)
    return jnp.sum(mixed.astype(F32), axis=0).astype(BF16)


def solution(mesh):
    in_specs = (
        P(None, "ctx"),
        P("ctx"),
        P("ctx", "head"),
        P("ctx", "head"),
        P("ctx", "head"),
        P("head", "ctx"),
        P("ctx", "head"),
        P("ctx", "head"),
        P("ctx"),
        P(),
        P("ctx", None, None),
        P("ctx", None, "head"),
        P(),
        P(),
        P(),
    )
    out_specs = P("head", "ctx")
    return jax.shard_map(shards, mesh=mesh, in_specs=in_specs, out_specs=out_specs, check_vma=False)
```
